128 devices in a mesh: rep: 8 (over x_lo, z), grp: 16 (over y, x_hi, core).
Axes of the slice: x: 4 (x_hi: 2, x_lo: 2; x = x_hi * 2 + x_lo), y: 4, z: 4, core: 2. Of those that a mesh axis runs over, the one named last changes fastest.
Arguments:
- master_weight: float32 [4096, 14336], P('rep', 'grp'), may hold values from -0.09375 to 0.09375
- first_moment: float32 [4096, 14336], P('rep', 'grp'), may hold values from -6 to 6
- second_moment: float32 [4096, 14336], P('rep', 'grp'), may hold values from 0.25 to 4
- prior_grad: float32 [4096, 14336], P('rep', 'grp'), may hold values from -6 to 6
- tokens: bfloat16 [16384, 4096], P(('rep', 'grp')), may hold values from -6 to 6
- cotangent: bfloat16 [16384, 14336], P(('rep', 'grp')), may hold values from -0.046875 to 0.046875
Outputs:
- new_master: float32 [4096, 14336], P('rep', 'grp')
- first_new: float32 [4096, 14336], P('rep', 'grp')
- second_new: float32 [4096, 14336], P('rep', 'grp')
- grad_sum: float32 [4096, 14336], P('rep', 'grp')
- up_proj: bfloat16 [16384, 14336], P(('rep', 'grp'))
The draws below stay inside these ranges and needn't reach their ends.
All inputs are finite; a program needn't handle non-finite values.
Results may differ from the reference program's by a relative error of at most 0.015.
Values may be sent and summed in bfloat16 or wider, within the bound.
A program may use at most 128 MiB of HBM per device.

```python
import math
import jax
import jax.numpy as jnp
from jax import lax

D = 4096
FF = 14336
STEP = 100
GROUPS = 8
GROUP_TOK = 2048
TOKENS = 16384


def shard_levels(rng, shape, shards, smallest, top_value):
    loudness = 1.0
    for position, parts in shards:
        heights = jax.random.uniform(jax.random.fold_in(jax.random.fold_in(rng, 6), position), (parts,), jnp.float32, smallest / len(shards), top_value / len(shards))
        loudness = loudness * jnp.repeat(jnp.exp(heights), shape[position] // parts).reshape((-1,) + (1,) * (len(shape) - 1 - position))
    return loudness


def noise(rng, shape, width, limit, pieces=(), dtype=jnp.bfloat16):
    loudness = shard_levels(rng, shape, pieces, -0.22, 0.18) if pieces else 1.0
    values = jax.random.normal(rng, shape, jnp.float32) * width * loudness
    return jnp.minimum(jnp.maximum(values, -limit), limit).astype(dtype)


def setup_inputs(seed: int = 0) -> dict:
    seeds = jax.random.split(jax.random.key(seed), 7)
    return {
        "master_weight": noise(seeds[0], (D, FF), D ** -0.5, 0.09375, ((0, 8), (1, 16)), jnp.float32),
        "first_moment": noise(seeds[1], (D, FF), 1.0, 6.0, ((0, 8), (1, 16)), jnp.float32),
        "second_moment": jnp.clip(jnp.exp(math.log(4.0) - 2.7725887 * jax.random.uniform(seeds[2], (D, FF), jnp.float32) ** shard_levels(seeds[2], (D, FF), ((0, 8), (1, 16)), -0.2, 0.2)), 0.25, 4.0),
        "prior_grad": noise(seeds[3], (D, FF), 1.0, 6.0, ((0, 8), (1, 16)), jnp.float32),
        "tokens": noise(seeds[4], (TOKENS, D), 1.0, 6.0, ((0, 128),)),
        "cotangent": noise(seeds[5], (TOKENS, FF), TOKENS ** -0.5, 0.046875, ((0, 128),)),
    }


learning_rate = 0.002
beta_one = 0.9
beta_two = 0.95
epsilon = 1e-08
decay_weight = 0.1

def adam_update(master_weight, first_moment, second_moment, prior_grad):
    first_new = beta_one * first_moment + (1.0 - beta_one) * prior_grad
    second_new = beta_two * second_moment + (1.0 - beta_two) * prior_grad * prior_grad
    bias_one = 1.0 - beta_one ** STEP
    bias_two = 1.0 - beta_two ** STEP
    step_size = first_new / bias_one / (jnp.sqrt(second_new / bias_two) + epsilon)
    new_master = master_weight - learning_rate * (step_size + decay_weight * master_weight)
    return (new_master, first_new, second_new)

def reference(master_weight, first_moment, second_moment, prior_grad, tokens, cotangent):
    new_master, first_new, second_new = adam_update(master_weight, first_moment, second_moment, prior_grad)
    weight_half = new_master.astype(jnp.bfloat16)
    token_groups = tokens.reshape(GROUPS, GROUP_TOK, D)
    back_groups = cotangent.reshape(GROUPS, GROUP_TOK, FF)

    def forward(block):
        return jnp.dot(block, weight_half, preferred_element_type=jnp.float32).astype(jnp.bfloat16)
    up_proj = lax.map(forward, token_groups).reshape(TOKENS, FF)

    def accumulate(total, pair):
        block, back_block = pair
        partial_value = jnp.dot(block.T, back_block, preferred_element_type=jnp.float32).astype(jnp.bfloat16)
        partial_value = lax.optimization_barrier(partial_value)
        return (total + partial_value.astype(jnp.float32), None)
    grad_sum, unused = lax.scan(accumulate, jnp.zeros((D, FF), jnp.float32), (token_groups, back_groups))
    return (new_master, first_new, second_new, grad_sum, up_proj)
```

```python
import functools

import jax
import jax.numpy as jnp
from jax import lax
from jax.experimental import pallas as pl
from jax.experimental.pallas import tpu as pltpu
from jax.sharding import PartitionSpec as P

STEP = 100

learning_rate = 0.002
beta_one = 0.9
beta_two = 0.95
epsilon = 1e-08
decay_weight = 0.1

MESH = pl.DeviceIdType.MESH
BF16, F32 = jnp.bfloat16, jnp.float32

ROWS = 128
WIDE = 4096
COLS = 896
PIECE = 512
PAIR = 2 * ROWS
GROUP = 16 * ROWS
QUARTER = 2 * PIECE
TILE = 256

PARTNERS = sorted(
    [(dy, dx, dc) for dy in range(4) for dx in range(2) for dc in range(2) if (dy, dx, dc) != (0, 0, 0)],
    key=lambda t: (-(min(t[0], 4 - t[0]) + 2 * t[1]), t),
)


def adam_update(master_weight, first_moment, second_moment, prior_grad):
    first_new = beta_one * first_moment + (1.0 - beta_one) * prior_grad
    second_new = beta_two * second_moment + (1.0 - beta_two) * prior_grad * prior_grad
    bias_one = 1.0 - beta_one**STEP
    bias_two = 1.0 - beta_two**STEP
    step_size = first_new / bias_one / (jnp.sqrt(second_new / bias_two) + epsilon)
    new_master = master_weight - learning_rate * (step_size + decay_weight * master_weight)
    return (new_master, first_new, second_new)


def kernel(
    w_in, tok_in, cot_in, grad_out, up_out,
    tok, wts, cot, acc, up, gsend, relay_in, zin, xsend, xin, gown,
    loc, cot_s, cot_r, out_s, out_r, tx_s, tx_r, ty_s, ty_r, tr_s, tr_r, ts_s, ts_r,
    wx_s, wx_r, wz_s, wz_r, wr_s, wr_r, g0_s, g0_r, gz_s, gz_r, gx_s, gx_r,
):
    rep, grp = lax.axis_index("rep"), lax.axis_index("grp")
    xl, z = rep // 4, rep % 4
    y, xh, c = grp // 4, (grp // 2) % 2, grp % 2

    def in_group(dy, dx, dc):
        return (rep, ((y + dy) % 4) * 4 + ((xh + dx) % 2) * 2 + (c + dc) % 2)

    def in_rep(dxl, dz):
        return (((xl + dxl) % 2) * 4 + (z + dz) % 4, grp)

    def rows_of(core, yy, half):
        return pl.multiple_of(((core * 4 + yy) * 2 + half) * ROWS, ROWS)

    sends = []

    def send(src, dst, ss, rs, to):
        copy = pltpu.make_async_remote_copy(src, dst, ss, rs, device_id=to, device_id_type=MESH)
        copy.start()
        sends.append(copy)

    def arrived(ref, rs):
        pltpu.make_async_remote_copy(ref, ref, rs, rs, device_id=in_group(0, 0, 1), device_id_type=MESH).wait_recv()

    barrier = pltpu.get_barrier_semaphore()
    peers = [in_group(*t) for t in PARTNERS] + [in_rep(0, 1), in_rep(0, 3), in_rep(1, 0)]
    for peer in peers:
        pl.semaphore_signal(barrier, inc=1, device_id=peer, device_id_type=MESH)
    pl.semaphore_wait(barrier, len(peers))

    own_rows = rows_of(c, y, xh)
    other_rows = rows_of(c, y, 1 - xh)
    places = [
        ((0, (z + 2) % 4), (1, (z + 2) % 4)),
        ((0, (z + 1) % 4), (0, (z + 3) % 4)),
        ((1, (z + 1) % 4), (1, (z + 3) % 4)),
        ((0, z), (1, z)),
    ]
    locals_ = {}
    for q in range(4):
        for h in range(2):
            a, zz = places[q][h]
            first = pl.multiple_of((a * 4 + zz) * PIECE, PIECE)
            locals_[q, h] = pltpu.make_async_copy(
                tok_in.at[:, pl.ds(first, PIECE)],
                tok.at[q, pl.ds(own_rows, ROWS), pl.ds(h * PIECE, PIECE)],
                loc.at[2 * q + h],
            )
            locals_[q, h].start()
    mine = pl.ds(pl.multiple_of(grp * COLS, 128), COLS)
    own_cot = pltpu.make_async_copy(cot_in.at[:, mine], cot.at[pl.ds(own_rows, ROWS)], loc.at[8])
    own_cot.start()
    own_w = pltpu.make_async_copy(
        w_in, wts.at[3, pl.ds(pl.multiple_of(xl * PIECE, PIECE), PIECE)], loc.at[9]
    )
    own_w.start()

    def exchange(q):
        locals_[q, 0].wait()
        locals_[q, 1].wait()
        own = tok.at[q, pl.ds(own_rows, ROWS)]
        send(own, own, tx_s.at[q], tx_r.at[q], in_group(0, 1, 0))

    exchange(0)

    def spread(order, block):
        src = wts.at[3, pl.ds(pl.multiple_of(block * PIECE, PIECE), PIECE)] if order else w_in
        send(src, wts.at[1 + block, pl.ds(PIECE, PIECE)], wz_s.at[order, 0], wz_r.at[order, 0], in_rep(0, 1))
        send(src, wts.at[1 + block, pl.ds(0, PIECE)], wz_s.at[order, 1], wz_r.at[order, 1], in_rep(0, 3))

    send(
        w_in, wts.at[3, pl.ds(pl.multiple_of(xl * PIECE, PIECE), PIECE)], wx_s.at[0], wx_r.at[0], in_rep(1, 0)
    )
    spread(0, xl)

    for i, t in enumerate(PARTNERS):
        to = in_group(*t)
        theirs = pl.ds(pl.multiple_of(to[1] * COLS, 128), COLS)
        send(cot_in.at[:, theirs], cot.at[pl.ds(own_rows, ROWS)], cot_s.at[i], cot_r.at[i], to)

    def pair_rows(core, dy):
        return pl.ds(rows_of(core, (y + dy) % 4, 0), PAIR)

    def half_rows(core, dy, half):
        return pl.ds(rows_of(core, (y + dy) % 4, half), ROWS)

    def to_sibling(q, rows, i):
        block = tok.at[q, rows]
        send(block, block, ts_s.at[q, i], ts_r.at[q, i], in_group(0, 0, 1))

    def step_a(q):
        arrived(tok.at[q, pl.ds(other_rows, ROWS)], tx_r.at[q])
        rows = pair_rows(c, 0)
        pair = tok.at[q, rows]
        send(pair, pair, ty_s.at[q, 0], ty_r.at[q, 0], in_group(1, 0, 0))
        send(pair, pair, ty_s.at[q, 1], ty_r.at[q, 1], in_group(3, 0, 0))
        to_sibling(q, rows, 0)

    def step_b(q):
        arrived(tok.at[q, pair_rows(c, 3)], ty_r.at[q, 0])
        onward = tok.at[q, half_rows(c, 3, 0)]
        send(onward, onward, tr_s.at[q, 0], tr_r.at[q, 0], in_group(1, 0, 0))
        arrived(tok.at[q, pair_rows(c, 1)], ty_r.at[q, 1])
        onward = tok.at[q, half_rows(c, 1, 1)]
        send(onward, onward, tr_s.at[q, 1], tr_r.at[q, 1], in_group(3, 0, 0))
        to_sibling(q, pair_rows(c, 3), 1)
        to_sibling(q, pair_rows(c, 1), 2)

    def step_c(q):
        for half in range(2):
            arrived(tok.at[q, half_rows(c, 2, half)], tr_r.at[q, half])
            to_sibling(q, half_rows(c, 2, half), 3 + half)

    def gathered(q):
        arrived(tok.at[q, pair_rows(1 - c, 0)], ts_r.at[q, 0])
        arrived(tok.at[q, pair_rows(1 - c, 3)], ts_r.at[q, 1])
        arrived(tok.at[q, pair_rows(1 - c, 1)], ts_r.at[q, 2])
        arrived(tok.at[q, half_rows(1 - c, 2, 0)], ts_r.at[q, 3])
        arrived(tok.at[q, half_rows(1 - c, 2, 1)], ts_r.at[q, 4])

    def weight_second():
        arrived(wts.at[3, pl.ds(pl.multiple_of((1 - xl) * PIECE, PIECE), PIECE)], wx_r.at[0])
        spread(1, 1 - xl)

    def weight_up():
        src = wts.at[1 + xl, pl.ds(PIECE, PIECE)]
        arrived(src, wz_r.at[0, 0])
        send(
            src, wts.at[0, pl.ds(pl.multiple_of(xl * PIECE, PIECE), PIECE)], wr_s.at[0], wr_r.at[0], in_rep(0, 1)
        )

    def weight_down():
        src = wts.at[2 - xl, pl.ds(0, PIECE)]
        arrived(src, wz_r.at[1, 1])
        send(
            src,
            wts.at[0, pl.ds(pl.multiple_of((1 - xl) * PIECE, PIECE), PIECE)],
            wr_s.at[1],
            wr_r.at[1],
            in_rep(0, 3),
        )

    def weight_rest():
        arrived(wts.at[1 + xl, pl.ds(0, PIECE)], wz_r.at[0, 1])
        arrived(wts.at[2 - xl, pl.ds(PIECE, PIECE)], wz_r.at[1, 0])
        arrived(wts.at[0, pl.ds(pl.multiple_of(xl * PIECE, PIECE), PIECE)], wr_r.at[0])
        arrived(wts.at[0, pl.ds(pl.multiple_of((1 - xl) * PIECE, PIECE), PIECE)], wr_r.at[1])
        own_w.wait()

    def grad_tile(q, first):
        return lax.dot_general(
            tok[q, :, pl.ds(first, TILE)], cot[...], (((0,), (0,)), ((), ())), preferred_element_type=F32
        )

    def grad_half(q, h, add=None):
        def tile(m, carry):
            here = pl.ds(pl.multiple_of(m * TILE, TILE), TILE)
            value = grad_tile(q, pl.multiple_of(h * PIECE + m * TILE, TILE))
            if add is not None:
                value = value + add[here, :].astype(F32)
            gsend[q, pl.ds(pl.multiple_of(h * PIECE + m * TILE, TILE), TILE), :] = value.astype(BF16)
            return carry

        lax.fori_loop(0, PIECE // TILE, tile, 0)

    def grad_zero():
        grad_half(0, 0)
        send(gsend.at[0, pl.ds(0, PIECE)], relay_in.at[0], g0_s.at[0], g0_r.at[0], in_rep(0, 1))
        grad_half(0, 1)
        send(gsend.at[0, pl.ds(PIECE, PIECE)], relay_in.at[1], g0_s.at[1], g0_r.at[1], in_rep(0, 3))

    def grad_neighbours(q):
        a = q - 1
        relayed = relay_in.at[a]

        def part(h):
            add = None
            if h == a:
                arrived(relayed, g0_r.at[a])
                add = relayed
            grad_half(q, h, add)
            send(
                gsend.at[q, pl.ds(h * PIECE, PIECE)],
                zin.at[a, h],
                gz_s.at[a, h],
                gz_r.at[a, h],
                in_rep(0, 3 if h else 1),
            )

        part(1 - a)
        part(a)

    def forward(q, last=False):
        def block(rows):
            value = jnp.dot(tok[q, rows, :], wts[q], preferred_element_type=F32)
            if q:
                value = value + acc[rows, :]
            if last:
                up[rows, :] = value.astype(BF16)
            else:
                acc[rows, :] = value

        def step(i, carry):
            block(pl.ds(pl.multiple_of(i * PAIR, PAIR), PAIR))
            return carry

        if not last:
            lax.fori_loop(0, GROUP // PAIR, step, 0)
            return
        for dy in (2, 1, 3, 0):
            for dc in range(2):
                core = (c + dc) % 2
                block(pair_rows(core, dy))
                for dx in (1, 0):
                    src = up.at[half_rows(core, dy, (xh + dx) % 2)]
                    if (dy, dx, dc) == (0, 0, 0):
                        own_up = pltpu.make_async_copy(src, up_out.at[:, mine], loc.at[10])
                        own_up.start()
                        locals_["up"] = own_up
                        continue
                    i = PARTNERS.index((dy, dx, dc))
                    send(src, up_out.at[:, mine], out_s.at[i], out_r.at[i], in_group(dy, dx, dc))

    def cotangent_here():
        own_cot.wait()
        for i, (dy, dx, dc) in enumerate(PARTNERS):
            place = pl.ds(rows_of((c - dc) % 2, (y - dy) % 4, (xh - dx) % 2), ROWS)
            arrived(cot.at[place], cot_r.at[i])

    exchange(1)
    step_a(0)
    exchange(2)
    weight_second()
    step_a(1)
    step_b(0)
    exchange(3)
    weight_up()
    step_a(2)
    step_b(1)
    step_c(0)
    weight_down()
    cotangent_here()
    gathered(0)
    grad_zero()
    step_a(3)
    step_b(2)
    step_c(1)
    weight_rest()
    forward(0)
    gathered(1)
    grad_neighbours(1)
    step_b(3)
    step_c(2)
    forward(1)
    gathered(2)
    grad_neighbours(2)
    step_c(3)
    forward(2)
    gathered(3)
    forward(3, last=True)

    def closing(a, store):
        def tile(m, carry):
            here = pl.ds(pl.multiple_of(m * TILE, TILE), TILE)
            value = grad_tile(3, pl.multiple_of(a * PIECE + m * TILE, TILE))
            value = value + zin[a, 0, here, :].astype(F32) + zin[a, 1, here, :].astype(F32)
            store(here, value)
            return carry

        lax.fori_loop(0, PIECE // TILE, tile, 0)

    def to_partner(here, value):
        xsend[here, :] = value.astype(BF16)

    def to_own(here, value):
        gown[here, :] = value

    for a in range(2):
        for h in range(2):
            arrived(zin.at[a, h], gz_r.at[a, h])
    closing(1 - xl, to_partner)
    send(xsend, xin, gx_s.at[0], gx_r.at[0], in_rep(1, 0))
    closing(xl, to_own)
    arrived(xin, gx_r.at[0])
    gown[...] = gown[...] + xin[...].astype(F32)
    result = pltpu.make_async_copy(gown, grad_out, loc.at[11])
    result.start()
    result.wait()
    for i, (dy, dx, dc) in enumerate(PARTNERS):
        source = ((y - dy) % 4) * 4 + ((xh - dx) % 2) * 2 + (c - dc) % 2
        arrived(up_out.at[:, pl.ds(pl.multiple_of(source * COLS, 128), COLS)], out_r.at[i])
    locals_["up"].wait()
    for copy in sends:
        copy.wait_send()


def exchange_and_multiply(weight_half, tokens, cotangent):
    dma = pltpu.SemaphoreType.DMA
    n = len(PARTNERS)
    return pl.pallas_call(
        kernel,
        out_shape=(
            jax.ShapeDtypeStruct((PIECE, COLS), F32),
            jax.ShapeDtypeStruct((ROWS, 16 * COLS), BF16),
        ),
        in_specs=[pl.BlockSpec(memory_space=pl.ANY)] * 3,
        out_specs=(pl.BlockSpec(memory_space=pl.ANY),) * 2,
        scratch_shapes=[
            pltpu.VMEM((4, GROUP, QUARTER), BF16),
            pltpu.VMEM((4, QUARTER, COLS), BF16),
            pltpu.VMEM((GROUP, COLS), BF16),
            pltpu.VMEM((GROUP, COLS), F32),
            pltpu.VMEM((GROUP, COLS), BF16),
            pltpu.VMEM((3, QUARTER, COLS), BF16),
            pltpu.VMEM((2, PIECE, COLS), BF16),
            pltpu.VMEM((2, 2, PIECE, COLS), BF16),
            pltpu.VMEM((PIECE, COLS), BF16),
            pltpu.VMEM((PIECE, COLS), BF16),
            pltpu.VMEM((PIECE, COLS), F32),
            dma((12,)),
            dma((n,)), dma((n,)),
            dma((n,)), dma((n,)),
            dma((4,)), dma((4,)),
            dma((4, 2)), dma((4, 2)),
            dma((4, 2)), dma((4, 2)),
            dma((4, 5)), dma((4, 5)),
            dma((1,)), dma((1,)),
            dma((2, 2)), dma((2, 2)),
            dma((2,)), dma((2,)),
            dma((2,)), dma((2,)),
            dma((2, 2)), dma((2, 2)),
            dma((1,)), dma((1,)),
        ],
        compiler_params=pltpu.CompilerParams(
            collective_id=0, has_side_effects=True, vmem_limit_bytes=62 * 2**20
        ),
        cost_estimate=pl.CostEstimate(
            flops=4 * GROUP * WIDE * COLS, bytes_accessed=16 * 2**20, transcendentals=0
        ),
        name="exchange_and_multiply",
    )(weight_half, tokens, cotangent)


def body(master_weight, first_moment, second_moment, prior_grad, tokens, cotangent):
    new_master, first_new, second_new = adam_update(
        master_weight, first_moment, second_moment, prior_grad
    )
    weight_half = new_master.astype(BF16)
    grad_sum, up_proj = exchange_and_multiply(weight_half, tokens, cotangent)
    return (new_master, first_new, second_new, grad_sum, up_proj)


def solution(mesh):
    return jax.shard_map(
        body,
        mesh=mesh,
        in_specs=(
            P("rep", "grp"),
            P("rep", "grp"),
            P("rep", "grp"),
            P("rep", "grp"),
            P(("rep", "grp"), None),
            P(("rep", "grp"), None),
        ),
        out_specs=(
            P("rep", "grp"),
            P("rep", "grp"),
            P("rep", "grp"),
            P("rep", "grp"),
            P(("rep", "grp"), None),
        ),
        check_vma=False,
    )
```

```python
import jax
import jax.numpy as jnp
from jax import lax
from jax.experimental import pallas as pl
from jax.experimental.pallas import tpu as pltpu
from jax.sharding import PartitionSpec as P

STEP = 100

learning_rate = 0.002
beta_one = 0.9
beta_two = 0.95
epsilon = 1e-08
decay_weight = 0.1

MESH = pl.DeviceIdType.MESH
BF16, F32 = jnp.bfloat16, jnp.float32

ROWS = 128
WIDE = 4096
COLS = 896
PIECE = 512
HALF = 256
PAIR = 2 * ROWS
GROUP = 16 * ROWS
QUARTER = 1024

PARTNERS = sorted(
    [(dy, dx, dc) for dy in range(4) for dx in range(2) for dc in range(2) if (dy, dx, dc) != (0, 0, 0)],
    key=lambda t: (-(min(t[0], 4 - t[0]) + 2 * t[1]), t),
)

SCHEDULE = (
    ("cotangent_far", 2),
    ("exchange", 2),
    ("cotangent_near",),
    ("exchange", 0),
    ("weight_across",),
    ("exchange", 1),
    ("weight_own",),
    ("cotangent_far", 3),
    ("weight_relay", 0),
    ("pair", 0),
    ("cotangent_far", 1),
    ("cotangent_far", 0),
    ("exchange", 3),
    ("pair", 2),
    ("gathered_own", 2),
    ("relay", 0),
    ("weight_second",),
    ("relay", 2),
    ("pair", 1),
    ("weight_relay", 1),
    ("share", 0),
    ("cotangent_wait",),
    ("weight_wait",),
    ("gathered_own", 0),
    ("gathered", 0),
    ("gradient", 0, 1),
    ("share", 2),
    ("gradient", 0, 0),
    ("pair", 3),
    ("gathered_own", 1),
    ("gathered", 2),
    ("gradient", 2, 0),
    ("forward", 0),
    ("gathered_own", 3),
    ("relay", 1),
    ("forward_own",),
    ("relay", 3),
    ("forward", 2),
    ("share", 1),
    ("gradient", 2, 1),
    ("gathered", 1),
    ("forward", 1),
    ("share", 3),
    ("gathered", 3),
    ("forward_last", 3),
    ("forward_last", 2),
    ("forward_last", 1),
    ("gradient", 1, 1),
    ("gradient", 1, 0),
    ("closing", 1),
    ("closing", 0),
)


def adam_update(master_weight, first_moment, second_moment, prior_grad):
    first_new = beta_one * first_moment + (1.0 - beta_one) * prior_grad
    second_new = beta_two * second_moment + (1.0 - beta_two) * prior_grad * prior_grad
    bias_one = 1.0 - beta_one**STEP
    bias_two = 1.0 - beta_two**STEP
    step_size = first_new / bias_one / (jnp.sqrt(second_new / bias_two) + epsilon)
    new_master = master_weight - learning_rate * (step_size + decay_weight * master_weight)
    return (new_master, first_new, second_new)


def kernel(
    w_in, tok_in, cot_in, grad_out, up_out,
    tok, wts, cot, acc, up, gsend, relay_in, zin, xsend, xin, gown,
    own_t, own_c, own_w, own_u, own_g,
    cot_s, cot_r, out_s, out_r, tx_s, tx_r, ty_s, ty_r, tr_s, tr_r, ts_s, ts_r,
    wx_s, wx_r, wz_s, wz_r, wr_s, wr_r, g0_s, g0_r, gz_s, gz_r, gx_s, gx_r,
):
    rep, grp = lax.axis_index("rep"), lax.axis_index("grp")
    xl, z = rep // 4, rep % 4
    y, xh, c = grp // 4, (grp // 2) % 2, grp % 2

    def in_group(dy, dx, dc):
        return (rep, ((y + dy) % 4) * 4 + ((xh + dx) % 2) * 2 + (c + dc) % 2)

    def in_rep(dxl, dz):
        return (((xl + dxl) % 2) * 4 + (z + dz) % 4, grp)

    sends = []

    def send(src, dst, ss, rs, to):
        copy = pltpu.make_async_remote_copy(src, dst, ss, rs, device_id=to, device_id_type=MESH)
        copy.start()
        sends.append(copy)

    def arrived(ref, rs):
        pltpu.make_async_remote_copy(
            ref, ref, rs, rs, device_id=in_group(0, 0, 1), device_id_type=MESH
        ).wait_recv()

    def row(core, dy, half):
        return pl.multiple_of(((core * 4 + (y + dy) % 4) * 2 + half) * ROWS, ROWS)

    def block_rows(core, dy, half):
        return pl.ds(row(core, dy, half), ROWS)

    def pair_rows(core, dy):
        return pl.ds(row(core, dy, 0), PAIR)

    def columns(device):
        return pl.ds(pl.multiple_of(device * COLS, 128), COLS)

    barrier = pltpu.get_barrier_semaphore()
    peers = [in_group(*t) for t in PARTNERS] + [in_rep(0, 1), in_rep(0, 3), in_rep(1, 0)]
    for peer in peers:
        pl.semaphore_signal(barrier, inc=1, device_id=peer, device_id_type=MESH)
    pl.semaphore_wait(barrier, len(peers))

    own = block_rows(c, 0, xh)
    own_tokens = {}
    for q in range(4):
        for h in range(2):
            zz = (z + (2, 1, 1, 0)[q] + (2 * h if q in (1, 2) else 0)) % 4
            hh = (h, 0, 1, h)[q]
            for a in range(2):
                copy = pltpu.make_async_copy(
                    tok_in.at[:, pl.ds(pl.multiple_of((a * 4 + zz) * PIECE + hh * HALF, HALF), HALF)],
                    tok.at[q, own, pl.ds(h * PIECE + a * HALF, HALF)],
                    own_t.at[q, 2 * h + a],
                )
                copy.start()
                own_tokens[q, h, a] = copy
    own_cot = pltpu.make_async_copy(cot_in.at[:, columns(grp)], cot.at[own], own_c.at[0])
    own_cot.start()
    own_weight = pltpu.make_async_copy(w_in, wts.at[3, :, xl], own_w.at[0])
    own_weight.start()
    own_up = pltpu.make_async_copy(up.at[own], up_out.at[:, columns(grp)], own_u.at[0])
    own_grad = [
        pltpu.make_async_copy(
            gown.at[pl.ds(h * HALF, HALF)], grad_out.at[pl.ds(h * HALF, HALF)], own_g.at[h]
        )
        for h in range(2)
    ]

    def to_sibling(q, rows, i):
        block = tok.at[q, rows]
        send(block, block, ts_s.at[q, i], ts_r.at[q, i], in_group(0, 0, 1))

    def exchange(q):
        for h in range(2):
            for a in range(2):
                own_tokens[q, h, a].wait()
        block = tok.at[q, own]
        send(block, block, tx_s.at[q], tx_r.at[q], in_group(0, 1, 0))

    def pair(q):
        arrived(tok.at[q, block_rows(c, 0, 1 - xh)], tx_r.at[q])
        block = tok.at[q, pair_rows(c, 0)]
        send(block, block, ty_s.at[q, 0], ty_r.at[q, 0], in_group(1, 0, 0))
        send(block, block, ty_s.at[q, 1], ty_r.at[q, 1], in_group(3, 0, 0))
        to_sibling(q, pair_rows(c, 0), 0)

    def relay(q):
        for i, back, to in ((0, 3, 1), (1, 1, 3)):
            arrived(tok.at[q, pair_rows(c, back)], ty_r.at[q, i])
            onward = tok.at[q, block_rows(c, back, i)]
            send(onward, onward, tr_s.at[q, i], tr_r.at[q, i], in_group(to, 0, 0))
        to_sibling(q, pair_rows(c, 3), 1)
        to_sibling(q, pair_rows(c, 1), 2)

    def share(q):
        for i in range(2):
            arrived(tok.at[q, block_rows(c, 2, i)], tr_r.at[q, i])
            to_sibling(q, block_rows(c, 2, i), 3 + i)

    def gathered_own(q):
        arrived(tok.at[q, pair_rows(1 - c, 0)], ts_r.at[q, 0])

    def gathered(q):
        for i, dy in ((1, 3), (2, 1)):
            arrived(tok.at[q, pair_rows(1 - c, dy)], ts_r.at[q, i])
        for i in range(2):
            arrived(tok.at[q, block_rows(1 - c, 2, i)], ts_r.at[q, 3 + i])

    def cotangent_to(i):
        to = in_group(*PARTNERS[i])
        send(cot_in.at[:, columns(to[1])], cot.at[own], cot_s.at[i], cot_r.at[i], to)

    def cotangent_near():
        for i, (dy, dx, dc) in enumerate(PARTNERS):
            if not dx:
                cotangent_to(i)

    def cotangent_far(far):
        for i, (dy, dx, dc) in enumerate(PARTNERS):
            if dx and dy == far:
                cotangent_to(i)

    def cotangent_wait():
        own_cot.wait()
        for i, (dy, dx, dc) in enumerate(PARTNERS):
            arrived(cot.at[block_rows((c - dc) % 2, -dy, (xh - dx) % 2)], cot_r.at[i])

    def spread(order, a):
        src = wts.at[3, :, a] if order else w_in
        send(src, wts.at[pl.ds(1, 2), 1, a], wz_s.at[order, 0], wz_r.at[order, 0], in_rep(0, 1))
        send(src, wts.at[pl.ds(1, 2), 0, a], wz_s.at[order, 1], wz_r.at[order, 1], in_rep(0, 3))

    def weight_own():
        spread(0, xl)

    def weight_across():
        send(w_in, wts.at[3, :, xl], wx_s.at[0], wx_r.at[0], in_rep(1, 0))

    def weight_second():
        arrived(wts.at[3, :, 1 - xl], wx_r.at[0])
        spread(1, 1 - xl)

    def weight_relay(order):
        a = 1 - xl if order else xl
        arrived(wts.at[pl.ds(1, 2), 1, a], wz_r.at[order, 0])
        send(wts.at[1, 1, a], wts.at[0, 0, a], wr_s.at[order, 0], wr_r.at[order, 0], in_rep(0, 1))
        arrived(wts.at[pl.ds(1, 2), 0, a], wz_r.at[order, 1])
        send(wts.at[2, 0, a], wts.at[0, 1, a], wr_s.at[order, 1], wr_r.at[order, 1], in_rep(0, 3))

    def weight_wait():
        for order in range(2):
            a = 1 - xl if order else xl
            for h in range(2):
                arrived(wts.at[0, h, a], wr_r.at[order, h])
        own_weight.wait()

    def gradient_tile(q, first):
        return lax.dot_general(
            tok[q, :, pl.ds(first, HALF)], cot[...], (((0,), (0,)), ((), ())), preferred_element_type=F32
        )

    def gradient_piece(q, h, add):
        def tile(m, carry):
            first = pl.multiple_of(h * PIECE + m * HALF, HALF)
            value = gradient_tile(q, first)
            if add is not None:
                value = value + add[pl.ds(pl.multiple_of(m * HALF, HALF), HALF), :].astype(F32)
            gsend[q, pl.ds(first, HALF), :] = value.astype(BF16)
            return carry

        lax.fori_loop(0, 2, tile, 0)

    def gradient(q, h):
        relayed = q == h + 1
        if relayed:
            arrived(relay_in.at[h], g0_r.at[h])
        gradient_piece(q, h, relay_in.at[h] if relayed else None)
        src, to = gsend.at[q, pl.ds(h * PIECE, PIECE)], in_rep(0, 3 if h else 1)
        if q:
            send(src, zin.at[q - 1, h], gz_s.at[q - 1, h], gz_r.at[q - 1, h], to)
        else:
            send(src, relay_in.at[h], g0_s.at[h], g0_r.at[h], to)

    def closing_tile(h, a):
        here = pl.ds(pl.multiple_of(a * HALF, HALF), HALF)
        value = gradient_tile(3, pl.multiple_of(h * PIECE + a * HALF, HALF))
        return value + zin[h, 0, here, :].astype(F32) + zin[h, 1, here, :].astype(F32)

    def closing(h):
        for i in range(2):
            arrived(zin.at[h, i], gz_r.at[h, i])
        here = pl.ds(h * HALF, HALF)
        xsend[here, :] = closing_tile(h, 1 - xl).astype(BF16)
        send(xsend.at[here], xin.at[here], gx_s.at[h], gx_r.at[h], in_rep(1, 0))
        gown[here, :] = closing_tile(h, xl)

    def forward_block(q, rows):
        return jnp.dot(tok[q, rows, :], wts[q].reshape(QUARTER, COLS), preferred_element_type=F32)

    def forward(q):
        def block(i, carry):
            rows = pair_rows(i // 3, 1 + i % 3)
            value = forward_block(q, rows)
            acc[rows, :] = value + acc[rows, :] if q else value
            return carry

        lax.fori_loop(0, 6, block, 0)

    def home(dy, dc):
        core = (c + dc) % 2
        for dx in (1, 0):
            if (dy, dx, dc) == (0, 0, 0):
                own_up.start()
                continue
            i = PARTNERS.index((dy, dx, dc))
            src = up.at[block_rows(core, dy, (xh + dx) % 2)]
            send(src, up_out.at[:, columns(grp)], out_s.at[i], out_r.at[i], in_group(dy, dx, dc))

    def forward_own():
        for dc in range(2):
            rows = pair_rows((c + dc) % 2, 0)
            up[rows, :] = sum(forward_block(q, rows) for q in range(4)).astype(BF16)
            home(0, dc)

    def forward_last(dy):
        for dc in range(2):
            rows = pair_rows((c + dc) % 2, dy)
            up[rows, :] = (forward_block(3, rows) + acc[rows, :]).astype(BF16)
            home(dy, dc)

    steps = {
        f.__name__: f
        for f in (
            exchange, pair, relay, share, gathered_own, gathered, cotangent_near, cotangent_far, cotangent_wait,
            weight_own, weight_across, weight_second, weight_relay, weight_wait,
            gradient, forward, forward_own, forward_last, closing,
        )
    }
    for name, *which in SCHEDULE:
        steps[name](*which)

    for h in range(2):
        here = pl.ds(h * HALF, HALF)
        arrived(xin.at[here], gx_r.at[h])
        gown[here, :] = gown[here, :] + xin[here, :].astype(F32)
        own_grad[h].start()
    for i, (dy, dx, dc) in enumerate(PARTNERS):
        source = ((y - dy) % 4) * 4 + ((xh - dx) % 2) * 2 + (c - dc) % 2
        arrived(up_out.at[:, columns(source)], out_r.at[i])
    own_up.wait()
    for copy in own_grad:
        copy.wait()
    for copy in sends:
        copy.wait_send()


def exchange_and_multiply(weight_half, tokens, cotangent):
    dma = pltpu.SemaphoreType.DMA
    n = len(PARTNERS)
    return pl.pallas_call(
        kernel,
        out_shape=(
            jax.ShapeDtypeStruct((PIECE, COLS), F32),
            jax.ShapeDtypeStruct((ROWS, 16 * COLS), BF16),
        ),
        in_specs=[pl.BlockSpec(memory_space=pl.ANY)] * 3,
        out_specs=(pl.BlockSpec(memory_space=pl.ANY),) * 2,
        scratch_shapes=[
            pltpu.VMEM((4, GROUP, QUARTER), BF16),
            pltpu.VMEM((4, 2, 2, HALF, COLS), BF16),
            pltpu.VMEM((GROUP, COLS), BF16),
            pltpu.VMEM((GROUP, COLS), F32),
            pltpu.VMEM((GROUP, COLS), BF16),
            pltpu.VMEM((3, QUARTER, COLS), BF16),
            pltpu.VMEM((2, PIECE, COLS), BF16),
            pltpu.VMEM((2, 2, PIECE, COLS), BF16),
            pltpu.VMEM((PIECE, COLS), BF16),
            pltpu.VMEM((PIECE, COLS), BF16),
            pltpu.VMEM((PIECE, COLS), F32),
            dma((4, 4)), dma((1,)), dma((1,)), dma((1,)), dma((2,)),
            dma((n,)), dma((n,)),
            dma((n,)), dma((n,)),
            dma((4,)), dma((4,)),
            dma((4, 2)), dma((4, 2)),
            dma((4, 2)), dma((4, 2)),
            dma((4, 5)), dma((4, 5)),
            dma((1,)), dma((1,)),
            dma((2, 2)), dma((2, 2)),
            dma((2, 2)), dma((2, 2)),
            dma((2,)), dma((2,)),
            dma((2, 2)), dma((2, 2)),
            dma((2,)), dma((2,)),
        ],
        compiler_params=pltpu.CompilerParams(
            collective_id=0, has_side_effects=True, vmem_limit_bytes=62 * 2**20
        ),
        cost_estimate=pl.CostEstimate(
            flops=4 * GROUP * WIDE * COLS, bytes_accessed=16 * 2**20, transcendentals=0
        ),
        name="exchange_and_multiply",
    )(weight_half.reshape(2, HALF, COLS), tokens, cotangent)


def body(master_weight, first_moment, second_moment, prior_grad, tokens, cotangent):
    new_master, first_new, second_new = adam_update(
        master_weight, first_moment, second_moment, prior_grad
    )
    weight_half = new_master.astype(BF16)
    grad_sum, up_proj = exchange_and_multiply(weight_half, tokens, cotangent)
    return (new_master, first_new, second_new, grad_sum, up_proj)


def solution(mesh):
    return jax.shard_map(
        body,
        mesh=mesh,
        in_specs=(
            P("rep", "grp"),
            P("rep", "grp"),
            P("rep", "grp"),
            P("rep", "grp"),
            P(("rep", "grp"), None),
            P(("rep", "grp"), None),
        ),
        out_specs=(
            P("rep", "grp"),
            P("rep", "grp"),
            P("rep", "grp"),
            P("rep", "grp"),
            P(("rep", "grp"), None),
        ),
        check_vma=False,
    )
```

```python
import jax
import jax.numpy as jnp
from jax import lax
from jax.experimental import pallas as pl
from jax.experimental.pallas import tpu as pltpu
from jax.sharding import PartitionSpec as P

STEP = 100

learning_rate = 0.002
beta_one = 0.9
beta_two = 0.95
epsilon = 1e-08
decay_weight = 0.1

MESH = pl.DeviceIdType.MESH
BF16, F32 = jnp.bfloat16, jnp.float32

ROWS = 128
WIDE = 4096
COLS = 896
PIECE = 512
HALF = 256
PAIR = 2 * ROWS
GROUP = 16 * ROWS
QUARTER = 1024

PARTNERS = sorted(
    [(dy, dx, dc) for dy in range(4) for dx in range(2) for dc in range(2) if (dy, dx, dc) != (0, 0, 0)],
    key=lambda t: (-(min(t[0], 4 - t[0]) + 2 * t[1]), t),
)

SCHEDULE = (
    ("cotangent_far", 2),
    ("exchange", 2),
    ("exchange", 0),
    ("weight_own",),
    ("weight_across",),
    ("cotangent_near",),
    ("pair", 0),
    ("exchange", 1),
    ("cotangent_far", 1),
    ("cotangent_far", 3),
    ("gathered_own", 0),
    ("weight_relay", 0),
    ("pair", 2),
    ("weight_second",),
    ("relay", 0),
    ("exchange", 3),
    ("cotangent_far", 0),
    ("weight_relay", 1),
    ("relay", 2),
    ("pair", 1),
    ("pair", 3),
    ("gathered_own", 2),
    ("cross", 2),
    ("gathered_near", 0),
    ("gathered_own", 1),
    ("weight_wait",),
    ("share", 0),
    ("gathered_own", 3),
    ("forward_own",),
    ("gathered_far", 0),
    ("cotangent_wait",),
    ("gradient", 0, 1),
    ("gradient", 0, 0),
    ("forward_near", 0),
    ("gathered_near", 2),
    ("relay", 1),
    ("share", 2),
    ("forward_far", 0),
    ("forward_near", 2),
    ("gathered_near", 1),
    ("relay", 3),
    ("cross", 1),
    ("forward_near", 1),
    ("gathered_near", 3),
    ("forward_last", 1),
    ("gathered_far", 2),
    ("forward_last", 3),
    ("share", 1),
    ("share", 3),
    ("gradient", 2, 1),
    ("gathered_far", 1),
    ("gradient", 2, 0),
    ("forward_far", 1),
    ("gathered_far", 3),
    ("forward_far", 2),
    ("gradient", 1, 0),
    ("closing_send", 1),
    ("forward_last", 2),
    ("gradient", 1, 1),
    ("closing_send", 0),
    ("closing_own", 1),
    ("closing_own", 0),
)

CROSSING = tuple(q for name, *(q, *_) in [(*step, 0) for step in SCHEDULE] if name == "cross")


def adam_update(master_weight, first_moment, second_moment, prior_grad):
    first_new = beta_one * first_moment + (1.0 - beta_one) * prior_grad
    second_new = beta_two * second_moment + (1.0 - beta_two) * prior_grad * prior_grad
    bias_one = 1.0 - beta_one**STEP
    bias_two = 1.0 - beta_two**STEP
    step_size = first_new / bias_one / (jnp.sqrt(second_new / bias_two) + epsilon)
    new_master = master_weight - learning_rate * (step_size + decay_weight * master_weight)
    return (new_master, first_new, second_new)


def kernel(
    w_in, tok_in, cot_in, grad_out, up_out,
    tok, wts, cot, acc, up, gsend, relay_in, zin, xsend, xin, gown,
    own_t, own_c, own_w, own_u, own_g,
    cot_s, cot_r, out_s, out_r, tx_s, tx_r, ty_s, ty_r, tr_s, tr_r, ts_s, ts_r,
    tc_s, tc_r, wx_s, wx_r, wz_s, wz_r, wr_s, wr_r, g0_s, g0_r, gz_s, gz_r, gx_s, gx_r,
):
    rep, grp = lax.axis_index("rep"), lax.axis_index("grp")
    xl, z = rep // 4, rep % 4
    y, xh, c = grp // 4, (grp // 2) % 2, grp % 2

    def in_group(dy, dx, dc):
        return (rep, ((y + dy) % 4) * 4 + ((xh + dx) % 2) * 2 + (c + dc) % 2)

    def in_rep(dxl, dz):
        return (((xl + dxl) % 2) * 4 + (z + dz) % 4, grp)

    sends = []

    def send(src, dst, ss, rs, to):
        copy = pltpu.make_async_remote_copy(src, dst, ss, rs, device_id=to, device_id_type=MESH)
        copy.start()
        sends.append(copy)

    def arrived(ref, rs):
        pltpu.make_async_remote_copy(
            ref, ref, rs, rs, device_id=in_group(0, 0, 1), device_id_type=MESH
        ).wait_recv()

    def row(core, dy, half):
        return pl.multiple_of(((core * 4 + (y + dy) % 4) * 2 + half) * ROWS, ROWS)

    def block_rows(core, dy, half):
        return pl.ds(row(core, dy, half), ROWS)

    def pair_rows(core, dy):
        return pl.ds(row(core, dy, 0), PAIR)

    def columns(device):
        return pl.ds(pl.multiple_of(device * COLS, 128), COLS)

    barrier = pltpu.get_barrier_semaphore()
    peers = [in_group(*t) for t in PARTNERS] + [in_rep(0, 1), in_rep(0, 3), in_rep(1, 0)]
    for peer in peers:
        pl.semaphore_signal(barrier, inc=1, device_id=peer, device_id_type=MESH)
    pl.semaphore_wait(barrier, len(peers))

    own = block_rows(c, 0, xh)
    own_tokens = {}
    for q in range(4):
        for h in range(2):
            zz = (z + (2, 1, 1, 0)[q] + (2 * h if q in (1, 2) else 0)) % 4
            hh = (h, 0, 1, h)[q]
            for a in range(2):
                copy = pltpu.make_async_copy(
                    tok_in.at[:, pl.ds(pl.multiple_of((a * 4 + zz) * PIECE + hh * HALF, HALF), HALF)],
                    tok.at[q, own, pl.ds(h * PIECE + a * HALF, HALF)],
                    own_t.at[q, 2 * h + a],
                )
                copy.start()
                own_tokens[q, h, a] = copy
    own_cot = pltpu.make_async_copy(cot_in.at[:, columns(grp)], cot.at[own], own_c.at[0])
    own_cot.start()
    own_weight = pltpu.make_async_copy(w_in, wts.at[3, :, xl], own_w.at[0])
    own_weight.start()
    own_up = pltpu.make_async_copy(up.at[own], up_out.at[:, columns(grp)], own_u.at[0])
    own_grad = [
        pltpu.make_async_copy(
            gown.at[pl.ds(h * HALF, HALF)], grad_out.at[pl.ds(h * HALF, HALF)], own_g.at[h]
        )
        for h in range(2)
    ]

    def to_sibling(q, rows, i):
        block = tok.at[q, rows]
        send(block, block, ts_s.at[q, i], ts_r.at[q, i], in_group(0, 0, 1))

    def exchange(q):
        for h in range(2):
            for a in range(2):
                own_tokens[q, h, a].wait()
        block = tok.at[q, own]
        send(block, block, tx_s.at[q], tx_r.at[q], in_group(0, 1, 0))

    def pair(q):
        arrived(tok.at[q, block_rows(c, 0, 1 - xh)], tx_r.at[q])
        block = tok.at[q, pair_rows(c, 0)]
        send(block, block, ty_s.at[q, 0], ty_r.at[q, 0], in_group(1, 0, 0))
        send(block, block, ty_s.at[q, 1], ty_r.at[q, 1], in_group(3, 0, 0))
        to_sibling(q, pair_rows(c, 0), 0)

    def from_opposite(q, i):
        if q in CROSSING:
            return pl.ds(pl.multiple_of(row(c, 2, xh) + i * (ROWS // 2), ROWS // 2), ROWS // 2)
        return block_rows(c, 2, i)

    def relay(q):
        for i, back, to in ((0, 3, 1), (1, 1, 3)):
            arrived(tok.at[q, pair_rows(c, back)], ty_r.at[q, i])
            if q in CROSSING:
                first = pl.multiple_of(row(c, back, xh) + i * (ROWS // 2), ROWS // 2)
                onward = tok.at[q, pl.ds(first, ROWS // 2)]
            else:
                onward = tok.at[q, block_rows(c, back, i)]
            send(onward, onward, tr_s.at[q, i], tr_r.at[q, i], in_group(to, 0, 0))
        to_sibling(q, pair_rows(c, 3), 1)
        to_sibling(q, pair_rows(c, 1), 2)

    def cross(q):
        for i in range(2):
            arrived(tok.at[q, from_opposite(q, i)], tr_r.at[q, i])
        block = tok.at[q, block_rows(c, 2, xh)]
        send(block, block, tc_s.at[q], tc_r.at[q], in_group(0, 1, 0))
        to_sibling(q, block_rows(c, 2, xh), 3)

    def share(q):
        if q in CROSSING:
            arrived(tok.at[q, block_rows(c, 2, 1 - xh)], tc_r.at[q])
            to_sibling(q, block_rows(c, 2, 1 - xh), 4)
            return
        for i in range(2):
            arrived(tok.at[q, from_opposite(q, i)], tr_r.at[q, i])
            to_sibling(q, block_rows(c, 2, i), 3 + i)

    def gathered_own(q):
        arrived(tok.at[q, pair_rows(1 - c, 0)], ts_r.at[q, 0])

    def gathered_near(q):
        for i, dy in ((1, 3), (2, 1)):
            arrived(tok.at[q, pair_rows(1 - c, dy)], ts_r.at[q, i])

    def gathered_far(q):
        if q in CROSSING:
            arrived(tok.at[q, block_rows(1 - c, 2, xh)], ts_r.at[q, 3])
            arrived(tok.at[q, block_rows(1 - c, 2, 1 - xh)], ts_r.at[q, 4])
        else:
            arrived(tok.at[q, block_rows(1 - c, 2, 0)], ts_r.at[q, 3])
            arrived(tok.at[q, block_rows(1 - c, 2, 1)], ts_r.at[q, 4])

    def cotangent_to(i):
        to = in_group(*PARTNERS[i])
        send(cot_in.at[:, columns(to[1])], cot.at[own], cot_s.at[i], cot_r.at[i], to)

    def cotangent_near():
        for i, (dy, dx, dc) in enumerate(PARTNERS):
            if not dx:
                cotangent_to(i)

    def cotangent_far(far):
        for i, (dy, dx, dc) in enumerate(PARTNERS):
            if dx and dy == far:
                cotangent_to(i)

    def cotangent_wait():
        own_cot.wait()
        for i, (dy, dx, dc) in enumerate(PARTNERS):
            arrived(cot.at[block_rows((c - dc) % 2, -dy, (xh - dx) % 2)], cot_r.at[i])

    def spread(order, a):
        src = wts.at[3, :, a] if order else w_in
        send(src, wts.at[pl.ds(1, 2), 1, a], wz_s.at[order, 0], wz_r.at[order, 0], in_rep(0, 1))
        send(src, wts.at[pl.ds(1, 2), 0, a], wz_s.at[order, 1], wz_r.at[order, 1], in_rep(0, 3))

    def weight_own():
        spread(0, xl)

    def weight_across():
        send(w_in, wts.at[3, :, xl], wx_s.at[0], wx_r.at[0], in_rep(1, 0))

    def weight_second():
        arrived(wts.at[3, :, 1 - xl], wx_r.at[0])
        spread(1, 1 - xl)

    def weight_relay(order):
        a = 1 - xl if order else xl
        arrived(wts.at[pl.ds(1, 2), 1, a], wz_r.at[order, 0])
        send(wts.at[1, 1, a], wts.at[0, 0, a], wr_s.at[order, 0], wr_r.at[order, 0], in_rep(0, 1))
        arrived(wts.at[pl.ds(1, 2), 0, a], wz_r.at[order, 1])
        send(wts.at[2, 0, a], wts.at[0, 1, a], wr_s.at[order, 1], wr_r.at[order, 1], in_rep(0, 3))

    def weight_wait():
        for order in range(2):
            a = 1 - xl if order else xl
            for h in range(2):
                arrived(wts.at[0, h, a], wr_r.at[order, h])
        own_weight.wait()

    def gradient_tile(q, first):
        return lax.dot_general(
            tok[q, :, pl.ds(first, HALF)], cot[...], (((0,), (0,)), ((), ())), preferred_element_type=F32
        )

    def rows_for(i):
        return pl.ds(pl.multiple_of((xl if i else 1 - xl) * HALF, HALF), HALF)

    def gradient(q, h):
        to = in_rep(0, 3 if h else 1)
        for i in range(2):
            here = rows_for(i)
            first = pl.multiple_of(h * PIECE + (xl if i else 1 - xl) * HALF, HALF)
            value = gradient_tile(q, first)
            if q == h + 1:
                arrived(relay_in.at[h, here], g0_r.at[h, i])
                value = value + relay_in[h, here, :].astype(F32)
            gsend[q, pl.ds(first, HALF), :] = value.astype(BF16)
            src = gsend.at[q, pl.ds(first, HALF)]
            if q:
                dst = zin.at[q - 1, h, here]
                send(src, dst, gz_s.at[q - 1, h, i], gz_r.at[q - 1, h, i], to)
            else:
                send(src, relay_in.at[h, here], g0_s.at[h, i], g0_r.at[h, i], to)

    def closing_tile(h, i):
        here = rows_for(i)
        for j in range(2):
            arrived(zin.at[h, j, here], gz_r.at[h, j, i])
        value = gradient_tile(3, pl.multiple_of(h * PIECE + (xl if i else 1 - xl) * HALF, HALF))
        return value + zin[h, 0, here, :].astype(F32) + zin[h, 1, here, :].astype(F32)

    def closing_send(h):
        here = pl.ds(h * HALF, HALF)
        xsend[here, :] = closing_tile(h, 0).astype(BF16)
        send(xsend.at[here], xin.at[here], gx_s.at[h], gx_r.at[h], in_rep(1, 0))

    def closing_own(h):
        gown[pl.ds(h * HALF, HALF), :] = closing_tile(h, 1)

    def forward_block(q, rows):
        return jnp.dot(tok[q, rows, :], wts[q].reshape(QUARTER, COLS), preferred_element_type=F32)

    def forward_rows(q, dys):
        def block(i, carry):
            rows = pair_rows(i // len(dys), dys[0] + 2 * (i % len(dys)))
            value = forward_block(q, rows)
            acc[rows, :] = value + acc[rows, :] if q else value
            return carry

        lax.fori_loop(0, 2 * len(dys), block, 0)

    def forward_near(q):
        forward_rows(q, (1, 3))

    def forward_far(q):
        forward_rows(q, (2,))

    def home(dy, dc):
        core = (c + dc) % 2
        for dx in (1, 0):
            if (dy, dx, dc) == (0, 0, 0):
                own_up.start()
                continue
            i = PARTNERS.index((dy, dx, dc))
            src = up.at[block_rows(core, dy, (xh + dx) % 2)]
            send(src, up_out.at[:, columns(grp)], out_s.at[i], out_r.at[i], in_group(dy, dx, dc))

    def forward_own():
        for dc in range(2):
            rows = pair_rows((c + dc) % 2, 0)
            up[rows, :] = sum(forward_block(q, rows) for q in range(4)).astype(BF16)
            home(0, dc)

    def forward_last(dy):
        for dc in range(2):
            rows = pair_rows((c + dc) % 2, dy)
            up[rows, :] = (forward_block(3, rows) + acc[rows, :]).astype(BF16)
            home(dy, dc)

    steps = {
        f.__name__: f
        for f in (
            exchange, pair, relay, cross, share, gathered_own, gathered_near, gathered_far, cotangent_near, cotangent_far, cotangent_wait,
            weight_own, weight_across, weight_second, weight_relay, weight_wait,
            gradient, forward_near, forward_far, forward_own, forward_last, closing_send, closing_own,
        )
    }
    for name, *which in SCHEDULE:
        steps[name](*which)

    for h in range(2):
        here = pl.ds(h * HALF, HALF)
        arrived(xin.at[here], gx_r.at[h])
        gown[here, :] = gown[here, :] + xin[here, :].astype(F32)
        own_grad[h].start()
    for i, (dy, dx, dc) in enumerate(PARTNERS):
        source = ((y - dy) % 4) * 4 + ((xh - dx) % 2) * 2 + (c - dc) % 2
        arrived(up_out.at[:, columns(source)], out_r.at[i])
    own_up.wait()
    for copy in own_grad:
        copy.wait()
    for copy in sends:
        copy.wait_send()


def exchange_and_multiply(weight_half, tokens, cotangent):
    dma = pltpu.SemaphoreType.DMA
    n = len(PARTNERS)
    return pl.pallas_call(
        kernel,
        out_shape=(
            jax.ShapeDtypeStruct((PIECE, COLS), F32),
            jax.ShapeDtypeStruct((ROWS, 16 * COLS), BF16),
        ),
        in_specs=[pl.BlockSpec(memory_space=pl.ANY)] * 3,
        out_specs=(pl.BlockSpec(memory_space=pl.ANY),) * 2,
        scratch_shapes=[
            pltpu.VMEM((4, GROUP, QUARTER), BF16),
            pltpu.VMEM((4, 2, 2, HALF, COLS), BF16),
            pltpu.VMEM((GROUP, COLS), BF16),
            pltpu.VMEM((GROUP, COLS), F32),
            pltpu.VMEM((GROUP, COLS), BF16),
            pltpu.VMEM((3, QUARTER, COLS), BF16),
            pltpu.VMEM((2, PIECE, COLS), BF16),
            pltpu.VMEM((2, 2, PIECE, COLS), BF16),
            pltpu.VMEM((PIECE, COLS), BF16),
            pltpu.VMEM((PIECE, COLS), BF16),
            pltpu.VMEM((PIECE, COLS), F32),
            dma((4, 4)), dma((1,)), dma((1,)), dma((1,)), dma((2,)),
            dma((n,)), dma((n,)),
            dma((n,)), dma((n,)),
            dma((4,)), dma((4,)),
            dma((4, 2)), dma((4, 2)),
            dma((4, 2)), dma((4, 2)),
            dma((4, 5)), dma((4, 5)),
            dma((4,)), dma((4,)),
            dma((1,)), dma((1,)),
            dma((2, 2)), dma((2, 2)),
            dma((2, 2)), dma((2, 2)),
            dma((2, 2)), dma((2, 2)),
            dma((2, 2, 2)), dma((2, 2, 2)),
            dma((2,)), dma((2,)),
        ],
        compiler_params=pltpu.CompilerParams(
            collective_id=0, has_side_effects=True, vmem_limit_bytes=62 * 2**20
        ),
        cost_estimate=pl.CostEstimate(
            flops=4 * GROUP * WIDE * COLS, bytes_accessed=16 * 2**20, transcendentals=0
        ),
        name="exchange_and_multiply",
    )(weight_half.reshape(2, HALF, COLS), tokens, cotangent)


def body(master_weight, first_moment, second_moment, prior_grad, tokens, cotangent):
    new_master, first_new, second_new = adam_update(
        master_weight, first_moment, second_moment, prior_grad
    )
    weight_half = new_master.astype(BF16)
    grad_sum, up_proj = exchange_and_multiply(weight_half, tokens, cotangent)
    return (new_master, first_new, second_new, grad_sum, up_proj)


def solution(mesh):
    return jax.shard_map(
        body,
        mesh=mesh,
        in_specs=(
            P("rep", "grp"),
            P("rep", "grp"),
            P("rep", "grp"),
            P("rep", "grp"),
            P(("rep", "grp"), None),
            P(("rep", "grp"), None),
        ),
        out_specs=(
            P("rep", "grp"),
            P("rep", "grp"),
            P("rep", "grp"),
            P("rep", "grp"),
            P(("rep", "grp"), None),
        ),
        check_vma=False,
    )
```

```python
import jax
import jax.numpy as jnp
from jax import lax
from jax.experimental import pallas as pl
from jax.experimental.pallas import tpu as pltpu
from jax.sharding import PartitionSpec as P

STEP = 100

learning_rate = 0.002
beta_one = 0.9
beta_two = 0.95
epsilon = 1e-08
decay_weight = 0.1
bias_one = 1.0 - beta_one**STEP
bias_two = 1.0 - beta_two**STEP

MESH = pl.DeviceIdType.MESH
BF16, F32 = jnp.bfloat16, jnp.float32

ROWS = 128
WIDE = 4096
COLS = 896
PIECE = 512
HALF = 256
PAIR = 2 * ROWS
GROUP = 16 * ROWS
QUARTER = 1024
STRIP = 32

PARTNERS = sorted(
    [(dy, dx, dc) for dy in range(4) for dx in range(2) for dc in range(2) if (dy, dx, dc) != (0, 0, 0)],
    key=lambda t: (-(min(t[0], 4 - t[0]) + 2 * t[1]), t),
)

SCHEDULE = (
    ("cotangent_far", 2),
    ("exchange", 2),
    ("exchange", 0),
    ("adam",),
    ("weight_own",),
    ("weight_across",),
    ("cotangent_near",),
    ("pair", 0),
    ("exchange", 1),
    ("cotangent_far", 1),
    ("cotangent_far", 3),
    ("gathered_own", 0),
    ("weight_relay", 0),
    ("pair", 2),
    ("weight_second",),
    ("relay", 0),
    ("exchange", 3),
    ("cotangent_far", 0),
    ("weight_relay", 1),
    ("relay", 2),
    ("pair", 1),
    ("pair", 3),
    ("gathered_own", 2),
    ("cross", 2),
    ("gathered_near", 0),
    ("gathered_own", 1),
    ("weight_wait",),
    ("share", 0),
    ("gathered_own", 3),
    ("forward_own",),
    ("gathered_far", 0),
    ("cotangent_wait",),
    ("gradient", 0, 1),
    ("gradient", 0, 0),
    ("forward_near", 0),
    ("gathered_near", 2),
    ("relay", 1),
    ("share", 2),
    ("forward_far", 0),
    ("forward_near", 2),
    ("gathered_near", 1),
    ("relay", 3),
    ("cross", 1),
    ("forward_near", 1),
    ("gathered_near", 3),
    ("forward_last", 1),
    ("gathered_far", 2),
    ("forward_last", 3),
    ("share", 1),
    ("share", 3),
    ("gradient", 2, 1),
    ("gathered_far", 1),
    ("gradient", 2, 0),
    ("forward_far", 1),
    ("gathered_far", 3),
    ("forward_far", 2),
    ("gradient", 1, 0),
    ("closing_send", 1),
    ("forward_last", 2),
    ("gradient", 1, 1),
    ("closing_send", 0),
    ("closing_own", 1),
    ("closing_own", 0),
)

CROSSING = tuple(q for name, *(q, *_) in [(*step, 0) for step in SCHEDULE] if name == "cross")


def kernel(
    master_in, first_in, second_in, prior_in, tok_in, cot_in,
    master, first_moment, second_moment, grad_out, up_out,
    tok, wts, cot, acc, up, gsend, relay_in, zin, xin,
    own_t, own_c, own_a, own_u,
    cot_s, cot_r, out_s, out_r, tx_s, tx_r, ty_s, ty_r, tr_s, tr_r, ts_s, ts_r,
    tc_s, tc_r, wx_s, wx_r, wz_s, wz_r, wr_s, wr_r, g0_s, g0_r, gz_s, gz_r, gx_s, gx_r,
):
    rep, grp = lax.axis_index("rep"), lax.axis_index("grp")
    xl, z = rep // 4, rep % 4
    y, xh, c = grp // 4, (grp // 2) % 2, grp % 2

    def in_group(dy, dx, dc):
        return (rep, ((y + dy) % 4) * 4 + ((xh + dx) % 2) * 2 + (c + dc) % 2)

    def in_rep(dxl, dz):
        return (((xl + dxl) % 2) * 4 + (z + dz) % 4, grp)

    sends = []

    def send(src, dst, ss, rs, to):
        copy = pltpu.make_async_remote_copy(src, dst, ss, rs, device_id=to, device_id_type=MESH)
        copy.start()
        sends.append(copy)
        return copy

    def arrived(ref, rs):
        pltpu.make_async_remote_copy(
            ref, ref, rs, rs, device_id=in_group(0, 0, 1), device_id_type=MESH
        ).wait_recv()

    def row(core, dy, half):
        return pl.multiple_of(((core * 4 + (y + dy) % 4) * 2 + half) * ROWS, ROWS)

    def block_rows(core, dy, half):
        return pl.ds(row(core, dy, half), ROWS)

    def pair_rows(core, dy):
        return pl.ds(row(core, dy, 0), PAIR)

    def columns(device):
        return pl.ds(pl.multiple_of(device * COLS, 128), COLS)

    own = block_rows(c, 0, xh)
    own_tokens = {}
    for q in range(4):
        for h in range(2):
            zz = (z + (2, 1, 1, 0)[q] + (2 * h if q in (1, 2) else 0)) % 4
            hh = (h, 0, 1, h)[q]
            for a in range(2):
                copy = pltpu.make_async_copy(
                    tok_in.at[:, pl.ds(pl.multiple_of((a * 4 + zz) * PIECE + hh * HALF, HALF), HALF)],
                    tok.at[q, own, pl.ds(h * PIECE + a * HALF, HALF)],
                    own_t.at[q, 2 * h + a],
                )
                copy.start()
                own_tokens[q, h, a] = copy
    own_cot = pltpu.make_async_copy(cot_in.at[:, columns(grp)], cot.at[own], own_c.at[0])
    own_cot.start()
    prior = acc.at[pl.ds(0, PIECE)]
    own_adam = [
        pltpu.make_async_copy(src, dst, own_a.at[i])
        for i, (src, dst) in enumerate(
            ((master_in, master), (first_in, first_moment), (second_in, second_moment), (prior_in, prior))
        )
    ]
    for copy in own_adam:
        copy.start()
    own_up = pltpu.make_async_copy(up.at[own], up_out.at[:, columns(grp)], own_u.at[0])

    barrier = pltpu.get_barrier_semaphore()
    peers = [in_group(*t) for t in PARTNERS] + [in_rep(0, 1), in_rep(0, 3), in_rep(1, 0)]
    for peer in peers:
        pl.semaphore_signal(barrier, inc=1, device_id=peer, device_id_type=MESH)
    pl.semaphore_wait(barrier, len(peers))

    def to_sibling(q, rows, i):
        block = tok.at[q, rows]
        send(block, block, ts_s.at[q, i], ts_r.at[q, i], in_group(0, 0, 1))

    def exchange(q):
        for h in range(2):
            for a in range(2):
                own_tokens[q, h, a].wait()
        block = tok.at[q, own]
        send(block, block, tx_s.at[q], tx_r.at[q], in_group(0, 1, 0))

    def pair(q):
        arrived(tok.at[q, block_rows(c, 0, 1 - xh)], tx_r.at[q])
        block = tok.at[q, pair_rows(c, 0)]
        send(block, block, ty_s.at[q, 0], ty_r.at[q, 0], in_group(1, 0, 0))
        send(block, block, ty_s.at[q, 1], ty_r.at[q, 1], in_group(3, 0, 0))
        to_sibling(q, pair_rows(c, 0), 0)

    def from_opposite(q, i):
        if q in CROSSING:
            return pl.ds(pl.multiple_of(row(c, 2, xh) + i * (ROWS // 2), ROWS // 2), ROWS // 2)
        return block_rows(c, 2, i)

    def relay(q):
        for i, back, to in ((0, 3, 1), (1, 1, 3)):
            arrived(tok.at[q, pair_rows(c, back)], ty_r.at[q, i])
            if q in CROSSING:
                first = pl.multiple_of(row(c, back, xh) + i * (ROWS // 2), ROWS // 2)
                onward = tok.at[q, pl.ds(first, ROWS // 2)]
            else:
                onward = tok.at[q, block_rows(c, back, i)]
            send(onward, onward, tr_s.at[q, i], tr_r.at[q, i], in_group(to, 0, 0))
        to_sibling(q, pair_rows(c, 3), 1)
        to_sibling(q, pair_rows(c, 1), 2)

    def cross(q):
        for i in range(2):
            arrived(tok.at[q, from_opposite(q, i)], tr_r.at[q, i])
        block = tok.at[q, block_rows(c, 2, xh)]
        send(block, block, tc_s.at[q], tc_r.at[q], in_group(0, 1, 0))
        to_sibling(q, block_rows(c, 2, xh), 3)

    def share(q):
        if q in CROSSING:
            arrived(tok.at[q, block_rows(c, 2, 1 - xh)], tc_r.at[q])
            to_sibling(q, block_rows(c, 2, 1 - xh), 4)
            return
        for i in range(2):
            arrived(tok.at[q, from_opposite(q, i)], tr_r.at[q, i])
            to_sibling(q, block_rows(c, 2, i), 3 + i)

    def gathered_own(q):
        arrived(tok.at[q, pair_rows(1 - c, 0)], ts_r.at[q, 0])

    def gathered_near(q):
        for i, dy in ((1, 3), (2, 1)):
            arrived(tok.at[q, pair_rows(1 - c, dy)], ts_r.at[q, i])

    def gathered_far(q):
        if q in CROSSING:
            arrived(tok.at[q, block_rows(1 - c, 2, xh)], ts_r.at[q, 3])
            arrived(tok.at[q, block_rows(1 - c, 2, 1 - xh)], ts_r.at[q, 4])
        else:
            arrived(tok.at[q, block_rows(1 - c, 2, 0)], ts_r.at[q, 3])
            arrived(tok.at[q, block_rows(1 - c, 2, 1)], ts_r.at[q, 4])

    def cotangent_to(i):
        to = in_group(*PARTNERS[i])
        send(cot_in.at[:, columns(to[1])], cot.at[own], cot_s.at[i], cot_r.at[i], to)

    def cotangent_near():
        for i, (dy, dx, dc) in enumerate(PARTNERS):
            if not dx:
                cotangent_to(i)

    def cotangent_far(far):
        for i, (dy, dx, dc) in enumerate(PARTNERS):
            if dx and dy == far:
                cotangent_to(i)

    def cotangent_wait():
        own_cot.wait()
        for i, (dy, dx, dc) in enumerate(PARTNERS):
            arrived(cot.at[block_rows((c - dc) % 2, -dy, (xh - dx) % 2)], cot_r.at[i])

    def adam():
        for copy in own_adam:
            copy.wait()
        for h in range(2):

            def some(i, carry):
                here = pl.ds(pl.multiple_of(h * HALF + i * STRIP, STRIP), STRIP)
                gradient = prior[here, :]
                weight = master[here, :]
                first_new = beta_one * first_moment[here, :] + (1.0 - beta_one) * gradient
                second_new = beta_two * second_moment[here, :] + (1.0 - beta_two) * gradient * gradient
                step_size = first_new / bias_one / (jnp.sqrt(second_new / bias_two) + epsilon)
                weight = weight - learning_rate * (step_size + decay_weight * weight)
                first_moment[here, :] = first_new
                second_moment[here, :] = second_new
                master[here, :] = weight
                wts[3, h, xl, pl.ds(pl.multiple_of(i * STRIP, STRIP), STRIP), :] = weight.astype(BF16)
                return carry

            lax.fori_loop(0, HALF // STRIP, some, 0)

    def spread(order, a):
        src = wts.at[3, :, a]
        send(src, wts.at[pl.ds(1, 2), 1, a], wz_s.at[order, 0], wz_r.at[order, 0], in_rep(0, 1))
        send(src, wts.at[pl.ds(1, 2), 0, a], wz_s.at[order, 1], wz_r.at[order, 1], in_rep(0, 3))

    def weight_own():
        spread(0, xl)

    def weight_across():
        block = wts.at[3, :, xl]
        send(block, block, wx_s.at[0], wx_r.at[0], in_rep(1, 0))

    def weight_second():
        arrived(wts.at[3, :, 1 - xl], wx_r.at[0])
        spread(1, 1 - xl)

    def weight_relay(order):
        a = 1 - xl if order else xl
        arrived(wts.at[pl.ds(1, 2), 1, a], wz_r.at[order, 0])
        send(wts.at[1, 1, a], wts.at[0, 0, a], wr_s.at[order, 0], wr_r.at[order, 0], in_rep(0, 1))
        arrived(wts.at[pl.ds(1, 2), 0, a], wz_r.at[order, 1])
        send(wts.at[2, 0, a], wts.at[0, 1, a], wr_s.at[order, 1], wr_r.at[order, 1], in_rep(0, 3))

    def weight_wait():
        for order in range(2):
            a = 1 - xl if order else xl
            for h in range(2):
                arrived(wts.at[0, h, a], wr_r.at[order, h])

    def gradient_tile(q, first):
        return lax.dot_general(
            tok[q, :, pl.ds(first, HALF)], cot[...], (((0,), (0,)), ((), ())), preferred_element_type=F32
        )

    def rows_for(i):
        return pl.ds(pl.multiple_of((xl if i else 1 - xl) * HALF, HALF), HALF)

    first_sends = {}

    def gradient(q, h):
        to = in_rep(0, 3 if h else 1)
        for i in range(2):
            here = rows_for(i)
            first = pl.multiple_of(h * PIECE + (xl if i else 1 - xl) * HALF, HALF)
            value = gradient_tile(q, first)
            if q == h + 1:
                arrived(relay_in.at[h, here], g0_r.at[h, i])
                value = value + relay_in[h, here, :].astype(F32)
            if q == 1:
                sends[:] = [copy for copy in sends if copy is not first_sends[h, i]]
                first_sends[h, i].wait_send()
            gsend[q // 2, pl.ds(first, HALF), :] = value.astype(BF16)
            src = gsend.at[q // 2, pl.ds(first, HALF)]
            if q:
                dst = zin.at[q - 1, h, here]
                send(src, dst, gz_s.at[q - 1, h, i], gz_r.at[q - 1, h, i], to)
            else:
                first_sends[h, i] = send(src, relay_in.at[h, here], g0_s.at[h, i], g0_r.at[h, i], to)

    def closing_tile(h, i):
        here = rows_for(i)
        for j in range(2):
            arrived(zin.at[h, j, here], gz_r.at[h, j, i])
        value = gradient_tile(3, pl.multiple_of(h * PIECE + (xl if i else 1 - xl) * HALF, HALF))
        return value + zin[h, 0, here, :].astype(F32) + zin[h, 1, here, :].astype(F32)

    def closing_send(h):
        out = relay_in.at[h, pl.ds(0, HALF)]
        out[...] = closing_tile(h, 0).astype(BF16)
        send(out, xin.at[pl.ds(h * HALF, HALF)], gx_s.at[h], gx_r.at[h], in_rep(1, 0))

    def closing_own(h):
        grad_out[pl.ds(h * HALF, HALF), :] = closing_tile(h, 1)

    def forward_block(q, rows):
        return jnp.dot(tok[q, rows, :], wts[q].reshape(QUARTER, COLS), preferred_element_type=F32)

    def acc_rows(core, dy):
        return pl.ds(pl.multiple_of((core * 3 + dy - 1) * PAIR, PAIR), PAIR)

    def forward_rows(q, dys):
        def block(i, carry):
            core, dy = i // len(dys), dys[0] + 2 * (i % len(dys))
            value = forward_block(q, pair_rows(core, dy))
            kept = acc_rows(core, dy)
            acc[kept, :] = value + acc[kept, :] if q else value
            return carry

        lax.fori_loop(0, 2 * len(dys), block, 0)

    def forward_near(q):
        forward_rows(q, (1, 3))

    def forward_far(q):
        forward_rows(q, (2,))

    def home(dy, dc):
        core = (c + dc) % 2
        for dx in (1, 0):
            if (dy, dx, dc) == (0, 0, 0):
                own_up.start()
                continue
            i = PARTNERS.index((dy, dx, dc))
            src = up.at[block_rows(core, dy, (xh + dx) % 2)]
            send(src, up_out.at[:, columns(grp)], out_s.at[i], out_r.at[i], in_group(dy, dx, dc))

    def forward_own():
        for dc in range(2):
            rows = pair_rows((c + dc) % 2, 0)
            up[rows, :] = sum(forward_block(q, rows) for q in range(4)).astype(BF16)
            home(0, dc)

    def forward_last(dy):
        for dc in range(2):
            core = (c + dc) % 2
            rows = pair_rows(core, dy)
            up[rows, :] = (forward_block(3, rows) + acc[acc_rows(core, dy), :]).astype(BF16)
            home(dy, dc)

    steps = {
        f.__name__: f
        for f in (
            exchange, pair, relay, cross, share, gathered_own, gathered_near, gathered_far, cotangent_near, cotangent_far, cotangent_wait,
            adam, weight_own, weight_across, weight_second, weight_relay, weight_wait,
            gradient, forward_near, forward_far, forward_own, forward_last, closing_send, closing_own,
        )
    }
    for name, *which in SCHEDULE:
        steps[name](*which)

    for h in range(2):
        here = pl.ds(h * HALF, HALF)
        arrived(xin.at[here], gx_r.at[h])
        grad_out[here, :] = grad_out[here, :] + xin[here, :].astype(F32)
    for i, (dy, dx, dc) in enumerate(PARTNERS):
        source = ((y - dy) % 4) * 4 + ((xh - dx) % 2) * 2 + (c - dc) % 2
        arrived(up_out.at[:, columns(source)], out_r.at[i])
    own_up.wait()
    for copy in sends:
        copy.wait_send()


def update_exchange_and_multiply(master, first_moment, second_moment, prior_grad, tokens, cotangent):
    dma = pltpu.SemaphoreType.DMA
    n = len(PARTNERS)
    shard = pltpu.VMEM((PIECE, COLS), F32)
    return pl.pallas_call(
        kernel,
        out_shape=(shard, shard, shard, shard, pltpu.VMEM((ROWS, 16 * COLS), BF16)),
        in_specs=[pl.BlockSpec(memory_space=pl.ANY)] * 6,
        out_specs=(pl.BlockSpec(memory_space=pltpu.VMEM),) * 5,
        scratch_shapes=[
            pltpu.VMEM((4, GROUP, QUARTER), BF16),
            pltpu.VMEM((4, 2, 2, HALF, COLS), BF16),
            pltpu.VMEM((GROUP, COLS), BF16),
            pltpu.VMEM((6 * PAIR, COLS), F32),
            pltpu.VMEM((GROUP, COLS), BF16),
            pltpu.VMEM((2, QUARTER, COLS), BF16),
            pltpu.VMEM((2, PIECE, COLS), BF16),
            pltpu.VMEM((2, 2, PIECE, COLS), BF16),
            pltpu.VMEM((PIECE, COLS), BF16),
            dma((4, 4)), dma((1,)), dma((4,)), dma((1,)),
            dma((n,)), dma((n,)),
            dma((n,)), dma((n,)),
            dma((4,)), dma((4,)),
            dma((4, 2)), dma((4, 2)),
            dma((4, 2)), dma((4, 2)),
            dma((4, 5)), dma((4, 5)),
            dma((4,)), dma((4,)),
            dma((1,)), dma((1,)),
            dma((2, 2)), dma((2, 2)),
            dma((2, 2)), dma((2, 2)),
            dma((2, 2)), dma((2, 2)),
            dma((2, 2, 2)), dma((2, 2, 2)),
            dma((2,)), dma((2,)),
        ],
        compiler_params=pltpu.CompilerParams(
            collective_id=0, has_side_effects=True, vmem_limit_bytes=53 * 2**20
        ),
        cost_estimate=pl.CostEstimate(
            flops=4 * GROUP * WIDE * COLS, bytes_accessed=16 * 2**20, transcendentals=0
        ),
        name="update_exchange_and_multiply",
    )(master, first_moment, second_moment, prior_grad, tokens, cotangent)


def solution(mesh):
    return jax.shard_map(
        update_exchange_and_multiply,
        mesh=mesh,
        in_specs=(
            P("rep", "grp"),
            P("rep", "grp"),
            P("rep", "grp"),
            P("rep", "grp"),
            P(("rep", "grp"), None),
            P(("rep", "grp"), None),
        ),
        out_specs=(
            P("rep", "grp"),
            P("rep", "grp"),
            P("rep", "grp"),
            P("rep", "grp"),
            P(("rep", "grp"), None),
        ),
        check_vma=False,
    )
```

```python
import jax
import jax.numpy as jnp
from jax import lax
from jax.experimental import pallas as pl
from jax.experimental.pallas import tpu as pltpu
from jax.sharding import PartitionSpec as P

STEP = 100

learning_rate = 0.002
beta_one = 0.9
beta_two = 0.95
epsilon = 1e-08
decay_weight = 0.1
bias_one = 1.0 - beta_one**STEP
bias_two = 1.0 - beta_two**STEP

MESH = pl.DeviceIdType.MESH
BF16, F32 = jnp.bfloat16, jnp.float32

ROWS = 128
WIDE = 4096
COLS = 896
PIECE = 512
HALF = 256
PAIR = 2 * ROWS
GROUP = 16 * ROWS
QUARTER = 1024
STRIP = 32

PARTNERS = sorted(
    [(dy, dx, dc) for dy in range(4) for dx in range(2) for dc in range(2) if (dy, dx, dc) != (0, 0, 0)],
    key=lambda t: (-(min(t[0], 4 - t[0]) + 2 * t[1]), t),
)

SCHEDULE = (
    ("cotangent_far", 2),
    ("cotangent_near",),
    ("exchange", 0),
    ("exchange", 1),
    ("adam",),
    ("weight_own",),
    ("weight_across",),
    ("weight_relay", 0),
    ("exchange", 2),
    ("exchange", 3),
    ("pair", 0),
    ("cotangent_far", 0),
    ("pair", 1),
    ("gathered_own", 0),
    ("weight_second",),
    ("relay", 0),
    ("cotangent_far", 3),
    ("relay", 1),
    ("cotangent_far", 1),
    ("pair", 3),
    ("gathered_own", 3),
    ("pair", 2),
    ("cross", 1),
    ("gathered_near", 0),
    ("weight_relay", 1),
    ("share", 0),
    ("gathered_own", 2),
    ("gathered_far", 0),
    ("weight_wait",),
    ("gathered_own", 1),
    ("forward_own",),
    ("forward_near", 0),
    ("cotangent_wait",),
    ("gradient", 0, 1),
    ("relay", 3),
    ("gathered_near", 1),
    ("gradient", 0, 0),
    ("forward_near", 1),
    ("gathered_near", 3),
    ("relay", 2),
    ("cross", 3),
    ("share", 1),
    ("gathered_near", 2),
    ("forward_near", 2),
    ("gathered_far", 1),
    ("forward_last", 1),
    ("gradient", 1, 1),
    ("forward_last", 3),
    ("gradient", 1, 0),
    ("forward_far", 0),
    ("share", 3),
    ("share", 2),
    ("gathered_far", 2),
    ("forward_far", 2),
    ("forward_far", 1),
    ("gathered_far", 3),
    ("closing_send", 0),
    ("forward_last", 2),
    ("gradient", 2, 0),
    ("gradient", 2, 1),
    ("closing_send", 1),
    ("closing_own", 1),
    ("closing_own", 0),
)

CROSSING = tuple(q for name, *(q, *_) in [(*step, 0) for step in SCHEDULE] if name == "cross")


def kernel(
    master_in, first_in, second_in, prior_in, tok_in, cot_in,
    master, first_moment, second_moment, grad_out, up_out,
    tok, wts, cot, acc, up, gsend, relay_in, zin, xin,
    own_t, own_c, own_a, own_u,
    cot_s, cot_r, out_s, out_r, tx_s, tx_r, ty_s, ty_r, tr_s, tr_r, ts_s, ts_r,
    tc_s, tc_r, wx_s, wx_r, wz_s, wz_r, wr_s, wr_r, g0_s, g0_r, gz_s, gz_r, gx_s, gx_r,
):
    rep, grp = lax.axis_index("rep"), lax.axis_index("grp")
    xl, z = rep // 4, rep % 4
    y, xh, c = grp // 4, (grp // 2) % 2, grp % 2

    def in_group(dy, dx, dc):
        return (rep, ((y + dy) % 4) * 4 + ((xh + dx) % 2) * 2 + (c + dc) % 2)

    def in_rep(dxl, dz):
        return (((xl + dxl) % 2) * 4 + (z + dz) % 4, grp)

    sends = []

    def send(src, dst, ss, rs, to):
        copy = pltpu.make_async_remote_copy(src, dst, ss, rs, device_id=to, device_id_type=MESH)
        copy.start()
        sends.append(copy)
        return copy

    def arrived(ref, rs):
        pltpu.make_async_remote_copy(
            ref, ref, rs, rs, device_id=in_group(0, 0, 1), device_id_type=MESH
        ).wait_recv()

    def row(core, dy, half):
        return pl.multiple_of(((core * 4 + (y + dy) % 4) * 2 + half) * ROWS, ROWS)

    def block_rows(core, dy, half):
        return pl.ds(row(core, dy, half), ROWS)

    def pair_rows(core, dy):
        return pl.ds(row(core, dy, 0), PAIR)

    def columns(device):
        return pl.ds(pl.multiple_of(device * COLS, 128), COLS)

    own = block_rows(c, 0, xh)
    own_tokens = {}
    for q in range(4):
        for h in range(2):
            zz = (z + (2, 1, 1, 0)[q] + (2 * h if q in (1, 2) else 0)) % 4
            hh = (h, 0, 1, h)[q]
            for a in range(2):
                copy = pltpu.make_async_copy(
                    tok_in.at[:, pl.ds(pl.multiple_of((a * 4 + zz) * PIECE + hh * HALF, HALF), HALF)],
                    tok.at[q, own, pl.ds(h * PIECE + a * HALF, HALF)],
                    own_t.at[q, 2 * h + a],
                )
                copy.start()
                own_tokens[q, h, a] = copy
    own_cot = pltpu.make_async_copy(cot_in.at[:, columns(grp)], cot.at[own], own_c.at[0])
    own_cot.start()
    prior = acc.at[pl.ds(0, PIECE)]
    own_adam = [
        pltpu.make_async_copy(src, dst, own_a.at[i])
        for i, (src, dst) in enumerate(
            ((master_in, master), (first_in, first_moment), (second_in, second_moment), (prior_in, prior))
        )
    ]
    for copy in own_adam:
        copy.start()
    own_up = pltpu.make_async_copy(up.at[own], up_out.at[:, columns(grp)], own_u.at[0])

    barrier = pltpu.get_barrier_semaphore()
    peers = [in_group(*t) for t in PARTNERS] + [in_rep(0, 1), in_rep(0, 3), in_rep(1, 0)]
    for peer in peers:
        pl.semaphore_signal(barrier, inc=1, device_id=peer, device_id_type=MESH)
    pl.semaphore_wait(barrier, len(peers))

    def to_sibling(q, rows, i):
        block = tok.at[q, rows]
        send(block, block, ts_s.at[q, i], ts_r.at[q, i], in_group(0, 0, 1))

    def exchange(q):
        for h in range(2):
            for a in range(2):
                own_tokens[q, h, a].wait()
        block = tok.at[q, own]
        send(block, block, tx_s.at[q], tx_r.at[q], in_group(0, 1, 0))

    def pair(q):
        arrived(tok.at[q, block_rows(c, 0, 1 - xh)], tx_r.at[q])
        block = tok.at[q, pair_rows(c, 0)]
        send(block, block, ty_s.at[q, 0], ty_r.at[q, 0], in_group(1, 0, 0))
        send(block, block, ty_s.at[q, 1], ty_r.at[q, 1], in_group(3, 0, 0))
        to_sibling(q, pair_rows(c, 0), 0)

    def from_opposite(q, i):
        if q in CROSSING:
            return pl.ds(pl.multiple_of(row(c, 2, xh) + i * (ROWS // 2), ROWS // 2), ROWS // 2)
        return block_rows(c, 2, i)

    def relay(q):
        for i, back, to in ((0, 3, 1), (1, 1, 3)):
            arrived(tok.at[q, pair_rows(c, back)], ty_r.at[q, i])
            if q in CROSSING:
                first = pl.multiple_of(row(c, back, xh) + i * (ROWS // 2), ROWS // 2)
                onward = tok.at[q, pl.ds(first, ROWS // 2)]
            else:
                onward = tok.at[q, block_rows(c, back, i)]
            send(onward, onward, tr_s.at[q, i], tr_r.at[q, i], in_group(to, 0, 0))
        to_sibling(q, pair_rows(c, 3), 1)
        to_sibling(q, pair_rows(c, 1), 2)

    def cross(q):
        for i in range(2):
            arrived(tok.at[q, from_opposite(q, i)], tr_r.at[q, i])
        block = tok.at[q, block_rows(c, 2, xh)]
        send(block, block, tc_s.at[q], tc_r.at[q], in_group(0, 1, 0))
        to_sibling(q, block_rows(c, 2, xh), 3)

    def share(q):
        if q in CROSSING:
            arrived(tok.at[q, block_rows(c, 2, 1 - xh)], tc_r.at[q])
            to_sibling(q, block_rows(c, 2, 1 - xh), 4)
            return
        for i in range(2):
            arrived(tok.at[q, from_opposite(q, i)], tr_r.at[q, i])
            to_sibling(q, block_rows(c, 2, i), 3 + i)

    def gathered_own(q):
        arrived(tok.at[q, pair_rows(1 - c, 0)], ts_r.at[q, 0])

    def gathered_near(q):
        for i, dy in ((1, 3), (2, 1)):
            arrived(tok.at[q, pair_rows(1 - c, dy)], ts_r.at[q, i])

    def gathered_far(q):
        if q in CROSSING:
            arrived(tok.at[q, block_rows(1 - c, 2, xh)], ts_r.at[q, 3])
            arrived(tok.at[q, block_rows(1 - c, 2, 1 - xh)], ts_r.at[q, 4])
        else:
            arrived(tok.at[q, block_rows(1 - c, 2, 0)], ts_r.at[q, 3])
            arrived(tok.at[q, block_rows(1 - c, 2, 1)], ts_r.at[q, 4])

    def cotangent_to(i):
        to = in_group(*PARTNERS[i])
        send(cot_in.at[:, columns(to[1])], cot.at[own], cot_s.at[i], cot_r.at[i], to)

    def cotangent_near():
        for i, (dy, dx, dc) in enumerate(PARTNERS):
            if not dx:
                cotangent_to(i)

    def cotangent_far(far):
        for i, (dy, dx, dc) in enumerate(PARTNERS):
            if dx and dy == far:
                cotangent_to(i)

    def cotangent_wait():
        own_cot.wait()
        for i, (dy, dx, dc) in enumerate(PARTNERS):
            arrived(cot.at[block_rows((c - dc) % 2, -dy, (xh - dx) % 2)], cot_r.at[i])

    def adam():
        for copy in own_adam:
            copy.wait()
        for h in range(2):

            def some(i, carry):
                here = pl.ds(pl.multiple_of(h * HALF + i * STRIP, STRIP), STRIP)
                gradient = prior[here, :]
                weight = master[here, :]
                first_new = beta_one * first_moment[here, :] + (1.0 - beta_one) * gradient
                second_new = beta_two * second_moment[here, :] + (1.0 - beta_two) * gradient * gradient
                step_size = first_new / bias_one / (jnp.sqrt(second_new / bias_two) + epsilon)
                weight = weight - learning_rate * (step_size + decay_weight * weight)
                first_moment[here, :] = first_new
                second_moment[here, :] = second_new
                master[here, :] = weight
                wts[3, h, xl, pl.ds(pl.multiple_of(i * STRIP, STRIP), STRIP), :] = weight.astype(BF16)
                return carry

            lax.fori_loop(0, HALF // STRIP, some, 0)

    def spread(order, a):
        src = wts.at[3, :, a]
        send(src, wts.at[pl.ds(1, 2), 1, a], wz_s.at[order, 0], wz_r.at[order, 0], in_rep(0, 1))
        send(src, wts.at[pl.ds(1, 2), 0, a], wz_s.at[order, 1], wz_r.at[order, 1], in_rep(0, 3))

    def weight_own():
        spread(0, xl)

    def weight_across():
        block = wts.at[3, :, xl]
        send(block, block, wx_s.at[0], wx_r.at[0], in_rep(1, 0))

    def weight_second():
        arrived(wts.at[3, :, 1 - xl], wx_r.at[0])
        spread(1, 1 - xl)

    def weight_relay(order):
        a = 1 - xl if order else xl
        arrived(wts.at[pl.ds(1, 2), 1, a], wz_r.at[order, 0])
        send(wts.at[1, 1, a], wts.at[0, 0, a], wr_s.at[order, 0], wr_r.at[order, 0], in_rep(0, 1))
        arrived(wts.at[pl.ds(1, 2), 0, a], wz_r.at[order, 1])
        send(wts.at[2, 0, a], wts.at[0, 1, a], wr_s.at[order, 1], wr_r.at[order, 1], in_rep(0, 3))

    def weight_wait():
        for order in range(2):
            a = 1 - xl if order else xl
            for h in range(2):
                arrived(wts.at[0, h, a], wr_r.at[order, h])

    def gradient_tile(q, first):
        return lax.dot_general(
            tok[q, :, pl.ds(first, HALF)], cot[...], (((0,), (0,)), ((), ())), preferred_element_type=F32
        )

    def rows_for(i):
        return pl.ds(pl.multiple_of((xl if i else 1 - xl) * HALF, HALF), HALF)

    first_sends = {}

    def gradient(q, h):
        to = in_rep(0, 3 if h else 1)
        for i in range(2):
            here = rows_for(i)
            first = pl.multiple_of(h * PIECE + (xl if i else 1 - xl) * HALF, HALF)
            value = gradient_tile(q, first)
            if q == h + 1:
                arrived(relay_in.at[h, here], g0_r.at[h, i])
                value = value + relay_in[h, here, :].astype(F32)
            if q == 1:
                sends[:] = [copy for copy in sends if copy is not first_sends[h, i]]
                first_sends[h, i].wait_send()
            gsend[q // 2, pl.ds(first, HALF), :] = value.astype(BF16)
            src = gsend.at[q // 2, pl.ds(first, HALF)]
            if q:
                dst = zin.at[q - 1, h, here]
                send(src, dst, gz_s.at[q - 1, h, i], gz_r.at[q - 1, h, i], to)
            else:
                first_sends[h, i] = send(src, relay_in.at[h, here], g0_s.at[h, i], g0_r.at[h, i], to)

    def closing_tile(h, i):
        here = rows_for(i)
        for j in range(2):
            arrived(zin.at[h, j, here], gz_r.at[h, j, i])
        value = gradient_tile(3, pl.multiple_of(h * PIECE + (xl if i else 1 - xl) * HALF, HALF))
        return value + zin[h, 0, here, :].astype(F32) + zin[h, 1, here, :].astype(F32)

    def closing_send(h):
        out = relay_in.at[h, pl.ds(0, HALF)]
        out[...] = closing_tile(h, 0).astype(BF16)
        send(out, xin.at[pl.ds(h * HALF, HALF)], gx_s.at[h], gx_r.at[h], in_rep(1, 0))

    def closing_own(h):
        grad_out[pl.ds(h * HALF, HALF), :] = closing_tile(h, 1)

    def forward_block(q, rows):
        return jnp.dot(tok[q, rows, :], wts[q].reshape(QUARTER, COLS), preferred_element_type=F32)

    def acc_rows(core, dy):
        return pl.ds(pl.multiple_of((core * 3 + dy - 1) * PAIR, PAIR), PAIR)

    def forward_rows(q, dys):
        def block(i, carry):
            core, dy = i // len(dys), dys[0] + 2 * (i % len(dys))
            value = forward_block(q, pair_rows(core, dy))
            kept = acc_rows(core, dy)
            acc[kept, :] = value + acc[kept, :] if q else value
            return carry

        lax.fori_loop(0, 2 * len(dys), block, 0)

    def forward_near(q):
        forward_rows(q, (1, 3))

    def forward_far(q):
        forward_rows(q, (2,))

    def home(dy, dc):
        core = (c + dc) % 2
        for dx in (1, 0):
            if (dy, dx, dc) == (0, 0, 0):
                own_up.start()
                continue
            i = PARTNERS.index((dy, dx, dc))
            src = up.at[block_rows(core, dy, (xh + dx) % 2)]
            send(src, up_out.at[:, columns(grp)], out_s.at[i], out_r.at[i], in_group(dy, dx, dc))

    def forward_own():
        for dc in range(2):
            rows = pair_rows((c + dc) % 2, 0)
            up[rows, :] = sum(forward_block(q, rows) for q in range(4)).astype(BF16)
            home(0, dc)

    def forward_last(dy):
        for dc in range(2):
            core = (c + dc) % 2
            rows = pair_rows(core, dy)
            up[rows, :] = (forward_block(3, rows) + acc[acc_rows(core, dy), :]).astype(BF16)
            home(dy, dc)

    steps = {
        f.__name__: f
        for f in (
            exchange, pair, relay, cross, share, gathered_own, gathered_near, gathered_far, cotangent_near, cotangent_far, cotangent_wait,
            adam, weight_own, weight_across, weight_second, weight_relay, weight_wait,
            gradient, forward_near, forward_far, forward_own, forward_last, closing_send, closing_own,
        )
    }
    for name, *which in SCHEDULE:
        steps[name](*which)

    for h in range(2):
        here = pl.ds(h * HALF, HALF)
        arrived(xin.at[here], gx_r.at[h])
        grad_out[here, :] = grad_out[here, :] + xin[here, :].astype(F32)
    for i, (dy, dx, dc) in enumerate(PARTNERS):
        source = ((y - dy) % 4) * 4 + ((xh - dx) % 2) * 2 + (c - dc) % 2
        arrived(up_out.at[:, columns(source)], out_r.at[i])
    own_up.wait()
    for copy in sends:
        copy.wait_send()


def update_exchange_and_multiply(master, first_moment, second_moment, prior_grad, tokens, cotangent):
    dma = pltpu.SemaphoreType.DMA
    n = len(PARTNERS)
    shard = pltpu.VMEM((PIECE, COLS), F32)
    return pl.pallas_call(
        kernel,
        out_shape=(shard, shard, shard, shard, pltpu.VMEM((ROWS, 16 * COLS), BF16)),
        in_specs=[pl.BlockSpec(memory_space=pl.ANY)] * 6,
        out_specs=(pl.BlockSpec(memory_space=pltpu.VMEM),) * 5,
        scratch_shapes=[
            pltpu.VMEM((4, GROUP, QUARTER), BF16),
            pltpu.VMEM((4, 2, 2, HALF, COLS), BF16),
            pltpu.VMEM((GROUP, COLS), BF16),
            pltpu.VMEM((6 * PAIR, COLS), F32),
            pltpu.VMEM((GROUP, COLS), BF16),
            pltpu.VMEM((2, QUARTER, COLS), BF16),
            pltpu.VMEM((2, PIECE, COLS), BF16),
            pltpu.VMEM((2, 2, PIECE, COLS), BF16),
            pltpu.VMEM((PIECE, COLS), BF16),
            dma((4, 4)), dma((1,)), dma((4,)), dma((1,)),
            dma((n,)), dma((n,)),
            dma((n,)), dma((n,)),
            dma((4,)), dma((4,)),
            dma((4, 2)), dma((4, 2)),
            dma((4, 2)), dma((4, 2)),
            dma((4, 5)), dma((4, 5)),
            dma((4,)), dma((4,)),
            dma((1,)), dma((1,)),
            dma((2, 2)), dma((2, 2)),
            dma((2, 2)), dma((2, 2)),
            dma((2, 2)), dma((2, 2)),
            dma((2, 2, 2)), dma((2, 2, 2)),
            dma((2,)), dma((2,)),
        ],
        compiler_params=pltpu.CompilerParams(
            collective_id=0, has_side_effects=True, vmem_limit_bytes=53 * 2**20
        ),
        cost_estimate=pl.CostEstimate(
            flops=4 * GROUP * WIDE * COLS, bytes_accessed=16 * 2**20, transcendentals=0
        ),
        name="update_exchange_and_multiply",
    )(master, first_moment, second_moment, prior_grad, tokens, cotangent)


def solution(mesh):
    return jax.shard_map(
        update_exchange_and_multiply,
        mesh=mesh,
        in_specs=(
            P("rep", "grp"),
            P("rep", "grp"),
            P("rep", "grp"),
            P("rep", "grp"),
            P(("rep", "grp"), None),
            P(("rep", "grp"), None),
        ),
        out_specs=(
            P("rep", "grp"),
            P("rep", "grp"),
            P("rep", "grp"),
            P("rep", "grp"),
            P(("rep", "grp"), None),
        ),
        check_vma=False,
    )
```
